32 devices in a mesh: row: 4 (over z), col: 4 (over y, x), depth: 2 (over core).
Axes of the slice: x: 2, y: 2, z: 4, core: 2. Of those that a mesh axis runs over, the one named last changes fastest.
Arguments:
- density: bfloat16 [2048, 2048], P('row', 'col'), may hold values from -1 to 1, as said below
- pattern: int32 [8, 8], replicated, may hold values from 0 to 1, as said below
- filter_pattern: int32 [8, 8], replicated, may hold values from 0 to 1, as said below
Outputs:
- square: bfloat16 [2048, 2048], P(('row', 'depth'), 'col')
The draws below stay inside these ranges and needn't reach their ends.
Inputs may be any that keep to these rules, and one draw needn't show every extreme that they name: density equals its transpose. 1 marks a stored block; the pattern is symmetric and every diagonal block is stored. `filter_pattern`: 1 marks a block that is kept; the pattern is symmetric and every diagonal block is kept.
All inputs are finite; a program needn't handle non-finite values.
Results may differ from the reference program's by a relative error of at most 0.001.
Values may be sent and summed in bfloat16 or wider, within the bound.
A program may use at most 64 MiB of HBM per device.

```python
import jax
import jax.numpy as jnp
from jax import lax

BS = 256
BLOCKS = 8
ORDER = 2048


def symmetric_mask(key, ones, of):
    coins = jax.random.randint(key, (BLOCKS, BLOCKS), 0, of)
    picked = (coins < ones).astype(jnp.int32)
    diagonal = jnp.eye(BLOCKS, dtype=jnp.int32)
    return jnp.maximum(jnp.maximum(picked, picked.T), diagonal)


def draw_density(key, part):
    first = jax.random.fold_in(key, 11)
    base = jax.random.normal(first, (ORDER, ORDER), jnp.float32) * 0.18
    values = (base + base.T) * 0.7071
    return jnp.clip(values, -1.0, 1.0).astype(jnp.bfloat16)


def draw_pattern(key, part):
    return symmetric_mask(jax.random.fold_in(key, 21), 3, 8)


def draw_filter_pattern(key, part):
    return symmetric_mask(jax.random.fold_in(key, 31), 1, 2)


def setup_inputs(seed: int = 0) -> dict:
    splits = jax.random.split(jax.random.key(seed), 4)
    return {
        "density": draw_density(jax.random.fold_in(splits[3], 71), 0),
        "pattern": draw_pattern(jax.random.fold_in(splits[3], 71), 0),
        "filter_pattern": draw_filter_pattern(jax.random.fold_in(splits[3], 71), 0),
    }


def reference(density, pattern, filter_pattern):
    blocked = density.reshape(BLOCKS, BS, BLOCKS, BS)
    kept = pattern[:, None, :, None] == 1
    matrix = jnp.where(kept, blocked, jnp.zeros((), density.dtype)).reshape(ORDER, ORDER)
    wide = matrix.astype(jnp.float32)
    full = jnp.dot(wide, wide, precision=lax.Precision.HIGHEST, preferred_element_type=jnp.float32)
    chosen = filter_pattern[:, None, :, None] == 1
    square = jnp.where(chosen, full.reshape(BLOCKS, BS, BLOCKS, BS), jnp.zeros((), jnp.float32))
    return square.reshape(ORDER, ORDER).astype(jnp.bfloat16)
```

```python
import functools

import jax
import jax.numpy as jnp
from jax import lax
from jax.experimental import pallas as pl
from jax.experimental.pallas import tpu as pltpu
from jax.sharding import PartitionSpec as P

BS = 256
PIECES = 2
MESH = pl.DeviceIdType.MESH


def kernel(grid, density, pattern, keep, out, left, right, total, *sems):
    (left_send, left_recv, up_send, down_send, right_recv, sib_send, sib_recv) = sems
    row = lax.axis_index("row")
    col = lax.axis_index("col")
    layer = lax.axis_index("depth")
    other = 1 - layer
    tile = density.shape[0]
    blocks = tile // BS
    half = tile // 2
    half_blocks = half // BS
    piece = half // PIECES

    barrier = pltpu.get_barrier_semaphore()

    def greet(device):
        pl.semaphore_signal(barrier, inc=1, device_id=device, device_id_type=MESH)

    for step in range(1, grid):
        greet((row, lax.rem(col + step, grid), layer))
    greet((row, col, other))

    @pl.when(row > 0)
    def _():
        greet((row - 1, col, layer))

    @pl.when(row < grid - 1)
    def _():
        greet((row + 1, col, layer))

    for i in range(blocks):
        for j in range(blocks):
            stored = pattern[row * blocks + i, col * blocks + j] == 1
            block = density[i * BS:(i + 1) * BS, j * BS:(j + 1) * BS]
            side, at = divmod(i, half_blocks)
            right[row, side, at * BS:(at + 1) * BS, j * BS:(j + 1) * BS] = jnp.where(
                stored, block, jnp.zeros_like(block)
            )

    ends = (row > 0).astype(jnp.int32) + (row < grid - 1).astype(jnp.int32)
    pl.semaphore_wait(barrier, grid + ends)

    def part(k, side, p):
        return right.at[k, side, pl.ds(p * piece, piece)]

    def upward(k, p):
        return pltpu.make_async_remote_copy(
            part(k, layer, p), part(k, layer, p), up_send.at[k, p], right_recv.at[k, p],
            device_id=(row + 1, col, layer), device_id_type=MESH,
        )

    def downward(k, p):
        return pltpu.make_async_remote_copy(
            part(k, layer, p), part(k, layer, p), down_send.at[k, p], right_recv.at[k, p],
            device_id=(row - 1, col, layer), device_id_type=MESH,
        )

    def across(k, p):
        return pltpu.make_async_remote_copy(
            part(k, layer, p), part(k, layer, p), sib_send.at[k, p], sib_recv.at[k, p],
            device_id=(row, col, other), device_id_type=MESH,
        )

    def from_across(k, p):
        return pltpu.make_async_remote_copy(
            part(k, other, p), part(k, other, p), sib_send.at[k, p], sib_recv.at[k, p],
            device_id=(row, col, other), device_id_type=MESH,
        )

    def along(step, slot):
        return pltpu.make_async_remote_copy(
            right.at[row, layer], left.at[slot], left_send.at[step], left_recv.at[slot],
            device_id=(row, lax.rem(col + step, grid), layer), device_id_type=MESH,
        )

    for p in range(PIECES):
        @pl.when(row < grid - 1)
        def _():
            upward(row, p).start()

        @pl.when(row > 0)
        def _():
            downward(row, p).start()

    for step in range(1, grid):
        along(step, col).start()

    left[col] = right[row, layer]

    total[...] = jnp.zeros_like(total)

    def multiply(k, remote):
        @pl.when(k != col)
        def _():
            along(0, k).wait_recv()

        if remote:
            for p in range(PIECES):
                from_across(k, p).wait_recv()
        for side in range(2):
            total[...] += jnp.dot(
                left[k, :, side * half:(side + 1) * half],
                right[k, side],
                preferred_element_type=jnp.float32,
            )

    def pass_on(step):
        for p in range(PIECES):
            @pl.when(row - step >= 0)
            def _():
                k = row - step
                upward(k, p).wait_recv()

                @pl.when(row < grid - 1)
                def _():
                    upward(k, p).start()

                across(k, p).start()

            @pl.when(row + step < grid)
            def _():
                k = row + step
                downward(k, p).wait_recv()

                @pl.when(row > 0)
                def _():
                    downward(k, p).start()

                across(k, p).start()

    def multiply_step(step):
        if step == 0:
            multiply(row, False)
            return

        @pl.when(row - step >= 0)
        def _():
            multiply(row - step, True)

        @pl.when(row + step < grid)
        def _():
            multiply(row + step, True)

    for step in range(1, grid):
        pass_on(step)
        multiply_step(step - 1)
    multiply_step(grid - 1)

    for i in range(half_blocks):
        for j in range(blocks):
            kept = keep[row * blocks + layer * half_blocks + i, col * blocks + j] == 1
            rows, cols = slice(i * BS, (i + 1) * BS), slice(j * BS, (j + 1) * BS)
            value = total[rows, cols]
            out[rows, cols] = jnp.where(kept, value, jnp.zeros_like(value)).astype(out.dtype)

    for step in range(1, grid):
        along(step, col).wait_send()
    for k in range(grid):
        for p in range(PIECES):
            @pl.when((row < grid - 1) & (k <= row))
            def _():
                upward(k, p).wait_send()

            @pl.when((row > 0) & (k >= row))
            def _():
                downward(k, p).wait_send()

            @pl.when(k != row)
            def _():
                across(k, p).wait_send()


def local(density, pattern, filter_pattern):
    grid = lax.axis_size("row")
    tile = density.shape[0]
    half = tile // 2
    dma = pltpu.SemaphoreType.DMA
    return pl.pallas_call(
        functools.partial(kernel, grid),
        out_shape=jax.ShapeDtypeStruct((half, tile), jnp.bfloat16),
        in_specs=[
            pl.BlockSpec(memory_space=pltpu.VMEM),
            pl.BlockSpec(memory_space=pltpu.SMEM),
            pl.BlockSpec(memory_space=pltpu.SMEM),
        ],
        out_specs=pl.BlockSpec(memory_space=pltpu.VMEM),
        scratch_shapes=[
            pltpu.VMEM((grid, half, tile), jnp.bfloat16),
            pltpu.VMEM((grid, 2, half, tile), jnp.bfloat16),
            pltpu.VMEM((half, tile), jnp.float32),
            dma((grid,)),
            dma((grid,)),
            dma((grid, PIECES)),
            dma((grid, PIECES)),
            dma((grid, PIECES)),
            dma((grid, PIECES)),
            dma((grid, PIECES)),
        ],
        compiler_params=pltpu.CompilerParams(
            collective_id=0, has_side_effects=True, vmem_limit_bytes=40 * 1024 * 1024
        ),
    )(density, pattern, filter_pattern)


def solution(mesh):
    return jax.shard_map(
        local,
        mesh=mesh,
        in_specs=(P("row", "col"), P(), P()),
        out_specs=P(("row", "depth"), "col"),
        check_vma=False,
    )
```

```python
import functools

import jax
import jax.numpy as jnp
from jax import lax
from jax.experimental import pallas as pl
from jax.experimental.pallas import tpu as pltpu
from jax.sharding import PartitionSpec as P

BS = 256
PIECES = 2
MESH = pl.DeviceIdType.MESH


def kernel(grid, density, pattern_ref, keep_ref, out, left, right, total, pattern, keep, *sems):
    (left_send, left_recv, up_send, down_send, right_recv, sib_send, sib_recv, load) = sems
    row = lax.axis_index("row")
    col = lax.axis_index("col")
    layer = lax.axis_index("depth")
    other = 1 - layer
    tile = density.shape[0]
    blocks = tile // BS
    half = tile // 2
    half_blocks = half // BS
    piece = half // PIECES

    loads = [
        pltpu.make_async_copy(density.at[pl.ds(side * half, half)], right.at[row, side], load.at[side])
        for side in range(2)
    ]
    loads.append(pltpu.make_async_copy(pattern_ref, pattern, load.at[2]))
    loads.append(pltpu.make_async_copy(keep_ref, keep, load.at[3]))
    for copy in loads:
        copy.start()

    barrier = pltpu.get_barrier_semaphore()

    def greet(device):
        pl.semaphore_signal(barrier, inc=1, device_id=device, device_id_type=MESH)

    for step in range(1, grid):
        greet((row, lax.rem(col + step, grid), layer))
    greet((row, col, other))

    @pl.when(row > 0)
    def _():
        greet((row - 1, col, layer))

    @pl.when(row < grid - 1)
    def _():
        greet((row + 1, col, layer))

    for copy in loads:
        copy.wait()
    for i in range(blocks):
        for j in range(blocks):
            stored = pattern[row * blocks + i, col * blocks + j] == 1
            side, at = divmod(i, half_blocks)
            rows, cols = slice(at * BS, (at + 1) * BS), slice(j * BS, (j + 1) * BS)
            block = right[row, side, rows, cols]
            right[row, side, rows, cols] = jnp.where(stored, block, jnp.zeros_like(block))

    ends = (row > 0).astype(jnp.int32) + (row < grid - 1).astype(jnp.int32)
    pl.semaphore_wait(barrier, grid + ends)

    def part(k, side, p):
        return right.at[k, side, pl.ds(p * piece, piece)]

    def upward(k, p):
        return pltpu.make_async_remote_copy(
            part(k, layer, p), part(k, layer, p), up_send.at[k, p], right_recv.at[k, p],
            device_id=(row + 1, col, layer), device_id_type=MESH,
        )

    def downward(k, p):
        return pltpu.make_async_remote_copy(
            part(k, layer, p), part(k, layer, p), down_send.at[k, p], right_recv.at[k, p],
            device_id=(row - 1, col, layer), device_id_type=MESH,
        )

    def across(k, p):
        return pltpu.make_async_remote_copy(
            part(k, layer, p), part(k, layer, p), sib_send.at[k, p], sib_recv.at[k, p],
            device_id=(row, col, other), device_id_type=MESH,
        )

    def from_across(k, p):
        return pltpu.make_async_remote_copy(
            part(k, other, p), part(k, other, p), sib_send.at[k, p], sib_recv.at[k, p],
            device_id=(row, col, other), device_id_type=MESH,
        )

    def along(step, slot):
        return pltpu.make_async_remote_copy(
            right.at[row, layer], left.at[slot], left_send.at[step], left_recv.at[slot],
            device_id=(row, lax.rem(col + step, grid), layer), device_id_type=MESH,
        )

    for p in range(PIECES):
        @pl.when(row < grid - 1)
        def _():
            upward(row, p).start()

        @pl.when(row > 0)
        def _():
            downward(row, p).start()

    for step in range(1, grid):
        along(step, col).start()

    left[col] = right[row, layer]

    total[...] = jnp.zeros_like(total)

    def multiply(k, remote):
        @pl.when(k != col)
        def _():
            along(0, k).wait_recv()

        if remote:
            for p in range(PIECES):
                from_across(k, p).wait_recv()
        for side in range(2):
            total[...] += jnp.dot(
                left[k, :, side * half:(side + 1) * half],
                right[k, side],
                preferred_element_type=jnp.float32,
            )

    def pass_on(step):
        for p in range(PIECES):
            @pl.when(row - step >= 0)
            def _():
                k = row - step
                upward(k, p).wait_recv()

                @pl.when(row < grid - 1)
                def _():
                    upward(k, p).start()

                across(k, p).start()

            @pl.when(row + step < grid)
            def _():
                k = row + step
                downward(k, p).wait_recv()

                @pl.when(row > 0)
                def _():
                    downward(k, p).start()

                across(k, p).start()

    def multiply_step(step):
        if step == 0:
            multiply(row, False)
            return

        @pl.when(row - step >= 0)
        def _():
            multiply(row - step, True)

        @pl.when(row + step < grid)
        def _():
            multiply(row + step, True)

    for step in range(1, grid):
        pass_on(step)
        multiply_step(step - 1)
    multiply_step(grid - 1)

    for i in range(half_blocks):
        for j in range(blocks):
            kept = keep[row * blocks + layer * half_blocks + i, col * blocks + j] == 1
            rows, cols = slice(i * BS, (i + 1) * BS), slice(j * BS, (j + 1) * BS)
            value = total[rows, cols]
            out[rows, cols] = jnp.where(kept, value, jnp.zeros_like(value)).astype(out.dtype)

    for step in range(1, grid):
        along(step, col).wait_send()
    for k in range(grid):
        for p in range(PIECES):
            @pl.when((row < grid - 1) & (k <= row))
            def _():
                upward(k, p).wait_send()

            @pl.when((row > 0) & (k >= row))
            def _():
                downward(k, p).wait_send()

            @pl.when(k != row)
            def _():
                across(k, p).wait_send()


def local(density, pattern, filter_pattern):
    grid = lax.axis_size("row")
    tile = density.shape[0]
    half = tile // 2
    dma = pltpu.SemaphoreType.DMA
    return pl.pallas_call(
        functools.partial(kernel, grid),
        out_shape=jax.ShapeDtypeStruct((half, tile), jnp.bfloat16),
        in_specs=[
            pl.BlockSpec(memory_space=pltpu.HBM),
            pl.BlockSpec(memory_space=pltpu.HBM),
            pl.BlockSpec(memory_space=pltpu.HBM),
        ],
        out_specs=pl.BlockSpec(memory_space=pltpu.VMEM),
        scratch_shapes=[
            pltpu.VMEM((grid, half, tile), jnp.bfloat16),
            pltpu.VMEM((grid, 2, half, tile), jnp.bfloat16),
            pltpu.VMEM((half, tile), jnp.float32),
            pltpu.SMEM(pattern.shape, pattern.dtype),
            pltpu.SMEM(filter_pattern.shape, filter_pattern.dtype),
            dma((grid,)),
            dma((grid,)),
            dma((grid, PIECES)),
            dma((grid, PIECES)),
            dma((grid, PIECES)),
            dma((grid, PIECES)),
            dma((grid, PIECES)),
            dma((4,)),
        ],
        compiler_params=pltpu.CompilerParams(
            collective_id=0, has_side_effects=True, vmem_limit_bytes=40 * 1024 * 1024
        ),
    )(density, pattern, filter_pattern)


def solution(mesh):
    return jax.shard_map(
        local,
        mesh=mesh,
        in_specs=(P("row", "col"), P(), P()),
        out_specs=P(("row", "depth"), "col"),
        check_vma=False,
    )
```

```python
import functools

import jax
import jax.numpy as jnp
from jax import lax
from jax.experimental import pallas as pl
from jax.experimental.pallas import tpu as pltpu
from jax.sharding import PartitionSpec as P

BS = 256
PIECES = 2
MESH = pl.DeviceIdType.MESH


def kernel(grid, density, pattern_ref, keep_ref, out, left, right, total, pattern, keep, *sems):
    (left_send, left_recv, up_send, down_send, right_recv, sib_send, sib_recv, load) = sems
    row = lax.axis_index("row")
    col = lax.axis_index("col")
    layer = lax.axis_index("depth")
    other = 1 - layer
    tile = density.shape[0]
    blocks = tile // BS
    half = tile // 2
    half_blocks = half // BS
    piece = half // PIECES

    loads = [
        pltpu.make_async_copy(density.at[pl.ds(side * half, half)], right.at[row, side], load.at[side])
        for side in range(2)
    ]
    loads.append(pltpu.make_async_copy(pattern_ref, pattern, load.at[2]))
    loads.append(pltpu.make_async_copy(keep_ref, keep, load.at[3]))
    for copy in loads:
        copy.start()

    barrier = pltpu.get_barrier_semaphore()

    def greet(device):
        pl.semaphore_signal(barrier, inc=1, device_id=device, device_id_type=MESH)

    for step in range(1, grid):
        greet((row, lax.rem(col + step, grid), layer))
    greet((row, col, other))

    @pl.when(row > 0)
    def _():
        greet((row - 1, col, layer))

    @pl.when(row < grid - 1)
    def _():
        greet((row + 1, col, layer))

    for copy in loads:
        copy.wait()
    for i in range(blocks):
        for j in range(blocks):
            stored = pattern[row * blocks + i, col * blocks + j] == 1
            side, at = divmod(i, half_blocks)
            rows, cols = slice(at * BS, (at + 1) * BS), slice(j * BS, (j + 1) * BS)
            block = right[row, side, rows, cols]
            right[row, side, rows, cols] = jnp.where(stored, block, jnp.zeros_like(block))

    ends = (row > 0).astype(jnp.int32) + (row < grid - 1).astype(jnp.int32)
    pl.semaphore_wait(barrier, grid + ends)

    def part(k, side, p):
        return right.at[k, side, pl.ds(p * piece, piece)]

    def upward(k, p):
        return pltpu.make_async_remote_copy(
            part(k, layer, p), part(k, layer, p), up_send.at[k, p], right_recv.at[k, p],
            device_id=(row + 1, col, layer), device_id_type=MESH,
        )

    def downward(k, p):
        return pltpu.make_async_remote_copy(
            part(k, layer, p), part(k, layer, p), down_send.at[k, p], right_recv.at[k, p],
            device_id=(row - 1, col, layer), device_id_type=MESH,
        )

    def across(k, p):
        return pltpu.make_async_remote_copy(
            part(k, layer, p), part(k, layer, p), sib_send.at[k, p], sib_recv.at[k, p],
            device_id=(row, col, other), device_id_type=MESH,
        )

    def from_across(k, p):
        return pltpu.make_async_remote_copy(
            part(k, other, p), part(k, other, p), sib_send.at[k, p], sib_recv.at[k, p],
            device_id=(row, col, other), device_id_type=MESH,
        )

    def along(step, slot):
        return pltpu.make_async_remote_copy(
            right.at[row, layer], left.at[slot], left_send.at[step], left_recv.at[slot],
            device_id=(row, lax.rem(col + step, grid), layer), device_id_type=MESH,
        )

    for p in range(PIECES):
        @pl.when(row < grid - 1)
        def _():
            upward(row, p).start()

        @pl.when(row > 0)
        def _():
            downward(row, p).start()

    for step in range(1, grid):
        along(step, col).start()

    left[col] = right[row, layer]

    total[...] = jnp.zeros_like(total)

    def multiply(k, remote):
        @pl.when(k != col)
        def _():
            along(0, k).wait_recv()

        if remote:
            for p in range(PIECES):
                from_across(k, p).wait_recv()
        for side in range(2):
            total[...] += jnp.dot(
                left[k, :, side * half:(side + 1) * half],
                right[k, side],
                preferred_element_type=jnp.float32,
            )

    def pass_on(step):
        for p in range(PIECES):
            @pl.when(row - step >= 0)
            def _():
                k = row - step
                upward(k, p).wait_recv()

                @pl.when(row < grid - 1)
                def _():
                    upward(k, p).start()

                across(k, p).start()

            @pl.when(row + step < grid)
            def _():
                k = row + step
                downward(k, p).wait_recv()

                @pl.when(row > 0)
                def _():
                    downward(k, p).start()

                across(k, p).start()

    def multiply_step(step):
        if step == 0:
            multiply(row, False)
            return

        @pl.when(row - step >= 0)
        def _():
            multiply(row - step, True)

        @pl.when(row + step < grid)
        def _():
            multiply(row + step, True)

    for step in range(1, grid):
        pass_on(step)
        multiply_step(step - 1)
    multiply_step(grid - 1)

    for i in range(half_blocks):
        for j in range(blocks):
            kept = keep[row * blocks + layer * half_blocks + i, col * blocks + j] == 1
            rows, cols = slice(i * BS, (i + 1) * BS), slice(j * BS, (j + 1) * BS)
            value = total[rows, cols]
            out[rows, cols] = jnp.where(kept, value, jnp.zeros_like(value)).astype(out.dtype)

    for step in range(1, grid):
        along(step, col).wait_send()
    for k in range(grid):
        for p in range(PIECES):
            @pl.when((row < grid - 1) & (k <= row))
            def _():
                upward(k, p).wait_send()

            @pl.when((row > 0) & (k >= row))
            def _():
                downward(k, p).wait_send()

            @pl.when(k != row)
            def _():
                across(k, p).wait_send()


def local(density, pattern, filter_pattern):
    grid = lax.axis_size("row")
    tile = density.shape[0]
    half = tile // 2
    dma = pltpu.SemaphoreType.DMA
    return pl.pallas_call(
        functools.partial(kernel, grid),
        out_shape=jax.ShapeDtypeStruct((half, tile), jnp.bfloat16),
        in_specs=[
            pl.BlockSpec(memory_space=pltpu.HBM),
            pl.BlockSpec(memory_space=pltpu.HBM),
            pl.BlockSpec(memory_space=pltpu.HBM),
        ],
        out_specs=pl.BlockSpec(memory_space=pltpu.VMEM),
        scratch_shapes=[
            pltpu.VMEM((grid, half, tile), jnp.bfloat16),
            pltpu.VMEM((grid, 2, half, tile), jnp.bfloat16),
            pltpu.VMEM((half, tile), jnp.float32),
            pltpu.SMEM(pattern.shape, pattern.dtype),
            pltpu.SMEM(filter_pattern.shape, filter_pattern.dtype),
            dma((grid,)),
            dma((grid,)),
            dma((grid, PIECES)),
            dma((grid, PIECES)),
            dma((grid, PIECES)),
            dma((grid, PIECES)),
            dma((grid, PIECES)),
            dma((4,)),
        ],
        compiler_params=pltpu.CompilerParams(
            collective_id=0, has_side_effects=True, vmem_limit_bytes=63 * 1024 * 1024
        ),
    )(density, pattern, filter_pattern)


def solution(mesh):
    return jax.shard_map(
        local,
        mesh=mesh,
        in_specs=(P("row", "col"), P(), P()),
        out_specs=P(("row", "depth"), "col"),
        check_vma=False,
    )
```

```python
import functools

import jax
import jax.numpy as jnp
from jax import lax
from jax.experimental import pallas as pl
from jax.experimental.pallas import tpu as pltpu
from jax.sharding import PartitionSpec as P

BS = 256
PIECES = 2
MESH = pl.DeviceIdType.MESH


def goes_up(n, k, c):
    d = lax.rem(c - k + n, n)
    near = (d > 0) & (2 * d < n)
    return (k == c) | (c == n - 1) | near | ((2 * d == n) & (k > 0)) | (2 * (c - k) > n)


def goes_down(n, k, c):
    return goes_up(n, n - 1 - k, n - 1 - c)


def by_chain(n, r, k, c):
    moves = ((k < r) & goes_up(n, k, c)) | ((k > r) & goes_down(n, k, c))
    return (r != c) & moves


def kernel(n, density, pattern_ref, keep_ref, out, left, right, total, pattern, keep, *sems):
    (left_send, pass_send, left_recv, up_send, down_send, extra_send, right_recv,
     sib_send, sib_recv, load) = sems
    row = lax.axis_index("row")
    col = lax.axis_index("col")
    layer = lax.axis_index("depth")
    other = 1 - layer
    tile = density.shape[0]
    blocks = tile // BS
    half = tile // 2
    half_blocks = half // BS
    piece = half // PIECES
    wide = max(w for w in range(1, n + 1) if n % w == 0 and w * w <= n)
    tall = n // wide
    my_y, my_x = lax.div(col, wide), lax.rem(col, wide)

    loads = [
        pltpu.make_async_copy(density.at[pl.ds(side * half, half)], right.at[row, side], load.at[side])
        for side in range(2)
    ]
    loads.append(pltpu.make_async_copy(pattern_ref, pattern, load.at[2]))
    loads.append(pltpu.make_async_copy(keep_ref, keep, load.at[3]))
    for copy in loads:
        copy.start()

    barrier = pltpu.get_barrier_semaphore()

    def greet(device):
        pl.semaphore_signal(barrier, inc=1, device_id=device, device_id_type=MESH)

    for step in range(1, n):
        greet((row, lax.rem(col + step, n), layer))
    greet((row, col, other))

    @pl.when(row > 0)
    def _():
        greet((row - 1, col, layer))

    @pl.when(row < n - 1)
    def _():
        greet((row + 1, col, layer))

    for copy in loads:
        copy.wait()
    for i in range(blocks):
        for j in range(blocks):
            stored = pattern[row * blocks + i, col * blocks + j] == 1
            side, at = divmod(i, half_blocks)
            rows, cols = slice(at * BS, (at + 1) * BS), slice(j * BS, (j + 1) * BS)
            block = right[row, side, rows, cols]
            right[row, side, rows, cols] = jnp.where(stored, block, jnp.zeros_like(block))

    ends = (row > 0).astype(jnp.int32) + (row < n - 1).astype(jnp.int32)
    pl.semaphore_wait(barrier, n + ends)

    up_open = (row < n - 1) & ((col != n - 1) | (row != n - 2))
    down_open = (row > 0) & ((col != 0) | (row != 1))
    corner = row == col

    def part(k, side, p):
        return right.at[k, side, pl.ds(p * piece, piece)]

    def left_part(k, p):
        return left.at[k, pl.ds(p * piece, piece)]

    def remote(src, dst, send, recv, device):
        return pltpu.make_async_remote_copy(
            src, dst, send, recv, device_id=device, device_id_type=MESH
        )

    def upward(k, p):
        ref = part(k, layer, p)
        return remote(ref, ref, up_send.at[k, p], right_recv.at[k, p], (row + 1, col, layer))

    def downward(k, p):
        ref = part(k, layer, p)
        return remote(ref, ref, down_send.at[k, p], right_recv.at[k, p], (row - 1, col, layer))

    def extra(k, p):
        return remote(
            part(k, layer, p), part(col, layer, p),
            extra_send.at[k, p], right_recv.at[col, p], (row, k, layer),
        )

    def arrived(k, p):
        return remote(
            part(k, layer, p), part(k, layer, p),
            extra_send.at[k, p], right_recv.at[k, p], (row, col, other),
        )

    def across(k, p):
        ref = part(k, layer, p)
        return remote(ref, ref, sib_send.at[k, p], sib_recv.at[k, p], (row, col, other))

    def left_across(k, p):
        return remote(
            left_part(k, p), part(k, layer, p),
            sib_send.at[k, p], sib_recv.at[k, p], (row, col, other),
        )

    def from_across(k, p):
        ref = part(k, other, p)
        return remote(ref, ref, sib_send.at[k, p], sib_recv.at[k, p], (row, col, other))

    def along(target, p):
        return remote(
            part(row, layer, p), left_part(col, p),
            left_send.at[target, p], left_recv.at[col, p], (row, target, layer),
        )

    def relay(k, target, slot, p):
        return remote(
            left_part(k, p), left_part(k, p),
            pass_send.at[k, slot, p], left_recv.at[k, p], (row, target, layer),
        )

    beside = [my_y * wide + lax.rem(my_x + i, wide) for i in range(1, wide)]
    above = [lax.rem(my_y + i, tall) * wide + my_x for i in range(1, tall)]
    diagonal = [
        lax.rem(my_y + i, tall) * wide + lax.rem(my_x + j, wide)
        for i in range(1, tall) for j in range(1, wide)
    ]

    def is_even(k):
        return lax.rem(lax.div(k, wide) + lax.rem(k, wide), 2) == 0

    for p in range(PIECES):
        @pl.when(up_open & goes_up(n, row, col))
        def _():
            upward(row, p).start()

        @pl.when(down_open & goes_down(n, row, col))
        def _():
            downward(row, p).start()

        for target in beside + above:
            along(target, p).start()

    left[col] = right[row, layer]
    total[...] = jnp.zeros_like(total)

    def take_left(k, p):
        left_copy = relay(k, col, 0, p)
        left_copy.wait_recv()

        @pl.when(corner)
        def _():
            left_across(k, p).start()

    def take_near(p):
        for k in beside:
            take_left(k, p)

            @pl.when(is_even(k))
            def _():
                for slot, target in enumerate(above):
                    relay(k, target, slot, p).start()

        for k in above:
            take_left(k, p)

            @pl.when(jnp.logical_not(is_even(k)))
            def _():
                for slot, target in enumerate(beside):
                    relay(k, target, slot, p).start()

    def hand_on(k, p):
        @pl.when(by_chain(n, row, k, col))
        def _():
            @pl.when(jnp.logical_not(by_chain(n, row, col, k)))
            def _():
                extra(k, p).start()

            across(k, p).start()

    def pass_on(step, p):
        @pl.when((row >= step) & goes_up(n, row - step, col) & ((col != n - 1) | (row != n - 1)))
        def _():
            k = row - step
            upward(k, p).wait_recv()

            @pl.when(up_open)
            def _():
                upward(k, p).start()

            hand_on(k, p)

        @pl.when((row + step < n) & goes_down(n, row + step, col) & ((col != 0) | (row != 0)))
        def _():
            k = row + step
            downward(k, p).wait_recv()

            @pl.when(down_open)
            def _():
                downward(k, p).start()

            hand_on(k, p)

    def has_extra(k):
        return (k != row) & (k != col) & (row != col) & jnp.logical_not(by_chain(n, row, k, col))

    def take_extra(step):
        @pl.when(lax.abs(row - col) == step)
        def _():
            for p in range(PIECES):
                for k in range(n):
                    @pl.when(has_extra(k))
                    def _():
                        arrived(k, p).wait_recv()
                        across(k, p).start()

    turned = (((1,), (1,)), ((), ()))

    def product(k, ref):
        return lax.dot_general(left[k], ref[...], turned, preferred_element_type=jnp.float32)

    def multiply(k):
        as_is = (k == row) | by_chain(n, row, k, col)

        @pl.when(as_is)
        def _():
            for side in range(2):
                total[...] += jnp.dot(
                    left[k, :, side * half:(side + 1) * half], right[k, side],
                    preferred_element_type=jnp.float32,
                )

        @pl.when(jnp.logical_not(as_is) & jnp.logical_not(corner))
        def _():
            for side in range(2):
                total[:, side * half:(side + 1) * half] += product(k, right.at[k, side])

        @pl.when(jnp.logical_not(as_is) & corner)
        def _():
            total[:, pl.ds(pl.multiple_of(layer * half, half), half)] += product(k, left.at[k])
            total[:, pl.ds(pl.multiple_of(other * half, half), half)] += product(k, right.at[k, other])

    for p in range(PIECES):
        pass_on(1, p)
        take_near(p)
    for step in range(2, n):
        for p in range(PIECES):
            pass_on(step, p)
        if step == 2:
            for p in range(PIECES):
                for k in diagonal:
                    take_left(k, p)
            multiply(row)
        take_extra(step - 1)
    take_extra(n - 1)

    @pl.loop(1, n)
    def _(step):
        k = lax.rem(row + step, n)
        for p in range(PIECES):
            from_across(k, p).wait_recv()
        multiply(k)

    for i in range(half_blocks):
        for j in range(blocks):
            kept = keep[row * blocks + layer * half_blocks + i, col * blocks + j] == 1
            rows, cols = slice(i * BS, (i + 1) * BS), slice(j * BS, (j + 1) * BS)
            value = total[rows, cols]
            out[rows, cols] = jnp.where(kept, value, jnp.zeros_like(value)).astype(out.dtype)

    for p in range(PIECES):
        for target in beside + above:
            along(target, p).wait_send()
        for k in beside:
            @pl.when(is_even(k))
            def _():
                for slot, target in enumerate(above):
                    relay(k, target, slot, p).wait_send()

        for k in above:
            @pl.when(jnp.logical_not(is_even(k)))
            def _():
                for slot, target in enumerate(beside):
                    relay(k, target, slot, p).wait_send()

        for k in range(n):
            @pl.when(up_open & (k <= row) & goes_up(n, k, col))
            def _():
                upward(k, p).wait_send()

            @pl.when(down_open & (k >= row) & goes_down(n, k, col))
            def _():
                downward(k, p).wait_send()

            @pl.when(k != row)
            def _():
                across(k, p).wait_send()

            @pl.when(by_chain(n, row, k, col) & jnp.logical_not(by_chain(n, row, col, k)))
            def _():
                extra(k, p).wait_send()


def local(density, pattern, filter_pattern):
    grid = lax.axis_size("row")
    tile = density.shape[0]
    half = tile // 2
    dma = pltpu.SemaphoreType.DMA
    return pl.pallas_call(
        functools.partial(kernel, grid),
        out_shape=jax.ShapeDtypeStruct((half, tile), jnp.bfloat16),
        in_specs=[
            pl.BlockSpec(memory_space=pltpu.HBM),
            pl.BlockSpec(memory_space=pltpu.HBM),
            pl.BlockSpec(memory_space=pltpu.HBM),
        ],
        out_specs=pl.BlockSpec(memory_space=pltpu.VMEM),
        scratch_shapes=[
            pltpu.VMEM((grid, half, tile), jnp.bfloat16),
            pltpu.VMEM((grid, 2, half, tile), jnp.bfloat16),
            pltpu.VMEM((half, tile), jnp.float32),
            pltpu.SMEM(pattern.shape, pattern.dtype),
            pltpu.SMEM(filter_pattern.shape, filter_pattern.dtype),
            dma((grid, PIECES)),
            dma((grid, grid, PIECES)),
            dma((grid, PIECES)),
            dma((grid, PIECES)),
            dma((grid, PIECES)),
            dma((grid, PIECES)),
            dma((grid, PIECES)),
            dma((grid, PIECES)),
            dma((grid, PIECES)),
            dma((4,)),
        ],
        compiler_params=pltpu.CompilerParams(
            collective_id=0, has_side_effects=True, vmem_limit_bytes=63 * 1024 * 1024
        ),
    )(density, pattern, filter_pattern)


def solution(mesh):
    return jax.shard_map(
        local,
        mesh=mesh,
        in_specs=(P("row", "col"), P(), P()),
        out_specs=P(("row", "depth"), "col"),
        check_vma=False,
    )
```

```python
import functools

import jax
import jax.numpy as jnp
from jax import lax
from jax.experimental import pallas as pl
from jax.experimental.pallas import tpu as pltpu
from jax.sharding import PartitionSpec as P

BS = 256
PIECES = 4
MESH = pl.DeviceIdType.MESH


def goes_up(n, k, c):
    d = lax.rem(c - k + n, n)
    near = (d > 0) & (2 * d < n)
    return (k == c) | (c == n - 1) | near | ((2 * d == n) & (k > 0)) | (2 * (c - k) > n)


def goes_down(n, k, c):
    return goes_up(n, n - 1 - k, n - 1 - c)


def by_chain(n, r, k, c):
    moves = ((k < r) & goes_up(n, k, c)) | ((k > r) & goes_down(n, k, c))
    return (r != c) & moves


def is_late(n, k, c):
    from_below = (k >= 2) & goes_up(n, k - 2, c)
    return (k >= 1) & goes_up(n, k, c) & goes_up(n, k - 1, c) & jnp.logical_not(from_below)


def tile_at(n, step, r, c):
    k = r - step
    early = jnp.where(is_late(n, k, c), k - 1, k)
    return jnp.where(is_late(n, k + 1, c), k + 1, early) if step > 1 else early


def kernel(n, density, pattern_ref, keep_ref, out, left, right, total, pattern, keep, *sems):
    (left_send, pass_send, left_recv, up_send, down_send, extra_send, right_recv,
     sib_send, sib_recv, load) = sems
    row = lax.axis_index("row")
    col = lax.axis_index("col")
    layer = lax.axis_index("depth")
    other = 1 - layer
    tile = density.shape[0]
    blocks = tile // BS
    half = tile // 2
    half_blocks = half // BS
    piece = half // PIECES
    wide = max(w for w in range(1, n + 1) if n % w == 0 and w * w <= n)
    tall = n // wide
    my_y, my_x = lax.div(col, wide), lax.rem(col, wide)

    loads = [
        pltpu.make_async_copy(density.at[pl.ds(side * half, half)], right.at[row, side], load.at[side])
        for side in range(2)
    ]
    loads.append(pltpu.make_async_copy(pattern_ref, pattern, load.at[2]))
    loads.append(pltpu.make_async_copy(keep_ref, keep, load.at[3]))
    for copy in loads:
        copy.start()

    barrier = pltpu.get_barrier_semaphore()

    def greet(device):
        pl.semaphore_signal(barrier, inc=1, device_id=device, device_id_type=MESH)

    for step in range(1, n):
        greet((row, lax.rem(col + step, n), layer))
    greet((row, col, other))

    @pl.when(row > 0)
    def _():
        greet((row - 1, col, layer))

    @pl.when(row < n - 1)
    def _():
        greet((row + 1, col, layer))

    for copy in loads:
        copy.wait()
    for i in range(blocks):
        for j in range(blocks):
            stored = pattern[row * blocks + i, col * blocks + j] == 1
            side, at = divmod(i, half_blocks)
            rows, cols = slice(at * BS, (at + 1) * BS), slice(j * BS, (j + 1) * BS)
            block = right[row, side, rows, cols]
            right[row, side, rows, cols] = jnp.where(stored, block, jnp.zeros_like(block))

    ends = (row > 0).astype(jnp.int32) + (row < n - 1).astype(jnp.int32)
    pl.semaphore_wait(barrier, n + ends)

    up_open = (row < n - 1) & ((col != n - 1) | (row != n - 2))
    down_open = (row > 0) & ((col != 0) | (row != 1))
    corner = row == col
    late_up = is_late(n, row, col)
    late_down = is_late(n, n - 1 - row, n - 1 - col)

    def part(k, side, p):
        return right.at[k, side, pl.ds(p * piece, piece)]

    def left_part(k, p):
        return left.at[k, pl.ds(p * piece, piece)]

    def remote(src, dst, send, recv, device):
        return pltpu.make_async_remote_copy(
            src, dst, send, recv, device_id=device, device_id_type=MESH
        )

    def upward(k, p):
        ref = part(k, layer, p)
        return remote(ref, ref, up_send.at[k, p], right_recv.at[k, p], (row + 1, col, layer))

    def downward(k, p):
        ref = part(k, layer, p)
        return remote(ref, ref, down_send.at[k, p], right_recv.at[k, p], (row - 1, col, layer))

    def extra(k, p):
        return remote(
            part(k, layer, p), part(col, layer, p),
            extra_send.at[k, p], right_recv.at[col, p], (row, k, layer),
        )

    def arrived(k, p):
        return remote(
            part(k, layer, p), part(k, layer, p),
            extra_send.at[k, p], right_recv.at[k, p], (row, col, other),
        )

    def across(k, p):
        ref = part(k, layer, p)
        return remote(ref, ref, sib_send.at[k, p], sib_recv.at[k, p], (row, col, other))

    def left_across(k, p):
        return remote(
            left_part(k, p), part(k, layer, p),
            sib_send.at[k, p], sib_recv.at[k, p], (row, col, other),
        )

    def from_across(k, p):
        ref = part(k, other, p)
        return remote(ref, ref, sib_send.at[k, p], sib_recv.at[k, p], (row, col, other))

    def along(target, p):
        return remote(
            part(row, layer, p), left_part(col, p),
            left_send.at[target, p], left_recv.at[col, p], (row, target, layer),
        )

    def relay(k, target, slot, p):
        return remote(
            left_part(k, p), left_part(k, p),
            pass_send.at[k, slot, p], left_recv.at[k, p], (row, target, layer),
        )

    beside = [my_y * wide + lax.rem(my_x + i, wide) for i in range(1, wide)]
    above = [lax.rem(my_y + i, tall) * wide + my_x for i in range(1, tall)]
    diagonal = [
        lax.rem(my_y + i, tall) * wide + lax.rem(my_x + j, wide)
        for i in range(1, tall) for j in range(1, wide)
    ]

    def is_even(k):
        return lax.rem(lax.div(k, wide) + lax.rem(k, wide), 2) == 0

    for p in range(PIECES):
        @pl.when(up_open & goes_up(n, row, col) & ((p == 0) | jnp.logical_not(late_up)))
        def _():
            upward(row, p).start()

        @pl.when(down_open & goes_down(n, row, col) & ((p == 0) | jnp.logical_not(late_down)))
        def _():
            downward(row, p).start()

        for target in beside + above:
            along(target, p).start()

    left[col] = right[row, layer]
    total[...] = jnp.zeros_like(total)

    def take_left(k, p):
        left_copy = relay(k, col, 0, p)
        left_copy.wait_recv()

        @pl.when(corner)
        def _():
            left_across(k, p).start()

    def take_near(p):
        for k in beside:
            take_left(k, p)

            @pl.when(is_even(k))
            def _():
                for slot, target in enumerate(above):
                    relay(k, target, slot, p).start()

        for k in above:
            take_left(k, p)

            @pl.when(jnp.logical_not(is_even(k)))
            def _():
                for slot, target in enumerate(beside):
                    relay(k, target, slot, p).start()

    def hand_on(k, p):
        @pl.when(by_chain(n, row, k, col))
        def _():
            @pl.when(jnp.logical_not(by_chain(n, row, col, k)))
            def _():
                extra(k, p).start()

            across(k, p).start()

    def pass_up(step, p):
        k = tile_at(n, step, row, col)

        @pl.when((k >= 0) & goes_up(n, k, col) & ((col != n - 1) | (row != n - 1)))
        def _():
            upward(k, p).wait_recv()

            @pl.when(up_open)
            def _():
                upward(k, p).start()

            hand_on(k, p)

    def pass_down(step, p):
        k = n - 1 - tile_at(n, step, n - 1 - row, n - 1 - col)

        @pl.when((k < n) & goes_down(n, k, col) & ((col != 0) | (row != 0)))
        def _():
            downward(k, p).wait_recv()

            @pl.when(down_open)
            def _():
                downward(k, p).start()

            hand_on(k, p)

    def send_late():
        @pl.when(up_open & goes_up(n, row, col) & late_up)
        def _():
            for p in range(1, PIECES):
                upward(row, p).start()

        @pl.when(down_open & goes_down(n, row, col) & late_down)
        def _():
            for p in range(1, PIECES):
                downward(row, p).start()

    def has_extra(k):
        return (k != row) & (k != col) & (row != col) & jnp.logical_not(by_chain(n, row, k, col))

    def take_extra(step):
        @pl.when(lax.abs(row - col) == step)
        def _():
            for p in range(PIECES):
                for k in range(n):
                    @pl.when(has_extra(k))
                    def _():
                        arrived(k, p).wait_recv()
                        across(k, p).start()

    turned = (((1,), (1,)), ((), ()))

    def product(k, ref):
        return lax.dot_general(left[k], ref[...], turned, preferred_element_type=jnp.float32)

    def multiply(k):
        as_is = (k == row) | by_chain(n, row, k, col)

        @pl.when(as_is)
        def _():
            for side in range(2):
                total[...] += jnp.dot(
                    left[k, :, side * half:(side + 1) * half], right[k, side],
                    preferred_element_type=jnp.float32,
                )

        @pl.when(jnp.logical_not(as_is) & jnp.logical_not(corner))
        def _():
            for side in range(2):
                total[:, side * half:(side + 1) * half] += product(k, right.at[k, side])

        @pl.when(jnp.logical_not(as_is) & corner)
        def _():
            total[:, pl.ds(pl.multiple_of(layer * half, half), half)] += product(k, left.at[k])
            total[:, pl.ds(pl.multiple_of(other * half, half), half)] += product(k, right.at[k, other])

    for p in range(PIECES):
        pass_up(1, p)
        pass_down(1, p)
        if p == PIECES - 1:
            send_late()
        take_near(p)
    for step in range(2, n):
        for p in range(PIECES):
            pass_up(step, p)
            pass_down(step, p)
        if step == 2:
            for p in range(PIECES):
                for k in diagonal:
                    take_left(k, p)
            multiply(row)
        take_extra(step - 1)
    take_extra(n - 1)

    @pl.loop(1, n)
    def _(step):
        k = lax.rem(row + step, n)
        for p in range(PIECES):
            from_across(k, p).wait_recv()
        multiply(k)

    for i in range(half_blocks):
        for j in range(blocks):
            kept = keep[row * blocks + layer * half_blocks + i, col * blocks + j] == 1
            rows, cols = slice(i * BS, (i + 1) * BS), slice(j * BS, (j + 1) * BS)
            value = total[rows, cols]
            out[rows, cols] = jnp.where(kept, value, jnp.zeros_like(value)).astype(out.dtype)

    for p in range(PIECES):
        for target in beside + above:
            along(target, p).wait_send()
        for k in beside:
            @pl.when(is_even(k))
            def _():
                for slot, target in enumerate(above):
                    relay(k, target, slot, p).wait_send()

        for k in above:
            @pl.when(jnp.logical_not(is_even(k)))
            def _():
                for slot, target in enumerate(beside):
                    relay(k, target, slot, p).wait_send()

        for k in range(n):
            @pl.when(up_open & (k <= row) & goes_up(n, k, col))
            def _():
                upward(k, p).wait_send()

            @pl.when(down_open & (k >= row) & goes_down(n, k, col))
            def _():
                downward(k, p).wait_send()

            @pl.when(k != row)
            def _():
                across(k, p).wait_send()

            @pl.when(by_chain(n, row, k, col) & jnp.logical_not(by_chain(n, row, col, k)))
            def _():
                extra(k, p).wait_send()


def local(density, pattern, filter_pattern):
    grid = lax.axis_size("row")
    tile = density.shape[0]
    half = tile // 2
    dma = pltpu.SemaphoreType.DMA
    return pl.pallas_call(
        functools.partial(kernel, grid),
        out_shape=jax.ShapeDtypeStruct((half, tile), jnp.bfloat16),
        in_specs=[
            pl.BlockSpec(memory_space=pltpu.HBM),
            pl.BlockSpec(memory_space=pltpu.HBM),
            pl.BlockSpec(memory_space=pltpu.HBM),
        ],
        out_specs=pl.BlockSpec(memory_space=pltpu.VMEM),
        scratch_shapes=[
            pltpu.VMEM((grid, half, tile), jnp.bfloat16),
            pltpu.VMEM((grid, 2, half, tile), jnp.bfloat16),
            pltpu.VMEM((half, tile), jnp.float32),
            pltpu.SMEM(pattern.shape, pattern.dtype),
            pltpu.SMEM(filter_pattern.shape, filter_pattern.dtype),
            dma((grid, PIECES)),
            dma((grid, grid, PIECES)),
            dma((grid, PIECES)),
            dma((grid, PIECES)),
            dma((grid, PIECES)),
            dma((grid, PIECES)),
            dma((grid, PIECES)),
            dma((grid, PIECES)),
            dma((grid, PIECES)),
            dma((4,)),
        ],
        compiler_params=pltpu.CompilerParams(
            collective_id=0, has_side_effects=True, vmem_limit_bytes=63 * 1024 * 1024
        ),
    )(density, pattern, filter_pattern)


def solution(mesh):
    return jax.shard_map(
        local,
        mesh=mesh,
        in_specs=(P("row", "col"), P(), P()),
        out_specs=P(("row", "depth"), "col"),
        check_vma=False,
    )
```

```python
import functools

import jax
import jax.numpy as jnp
from jax import lax
from jax.experimental import pallas as pl
from jax.experimental.pallas import tpu as pltpu
from jax.sharding import PartitionSpec as P

BS = 256
PIECES = 2
MESH = pl.DeviceIdType.MESH


def kernel(n, density, pattern_ref, keep_ref, out, left, right, total, pattern, keep, *sems):
    (left_send, pass_send, left_recv, up_send, down_send, right_recv,
     sib_send, sib_recv, load) = sems
    row = lax.axis_index("row")
    col = lax.axis_index("col")
    layer = lax.axis_index("depth")
    other = 1 - layer
    tile = density.shape[0]
    blocks = tile // BS
    half = tile // 2
    half_blocks = half // BS
    piece = half // PIECES
    wide = max(w for w in range(1, n + 1) if n % w == 0 and w * w <= n)
    tall = n // wide
    my_y, my_x = lax.div(col, wide), lax.rem(col, wide)

    loads = [
        pltpu.make_async_copy(density.at[pl.ds(side * half, half)], right.at[row, side], load.at[side])
        for side in range(2)
    ]
    loads.append(pltpu.make_async_copy(pattern_ref, pattern, load.at[2]))
    loads.append(pltpu.make_async_copy(keep_ref, keep, load.at[3]))
    for copy in loads:
        copy.start()

    barrier = pltpu.get_barrier_semaphore()

    def greet(device):
        pl.semaphore_signal(barrier, inc=1, device_id=device, device_id_type=MESH)

    for step in range(1, n):
        greet((row, lax.rem(col + step, n), layer))
    greet((row, col, other))

    @pl.when(row > 0)
    def _():
        greet((row - 1, col, layer))

    @pl.when(row < n - 1)
    def _():
        greet((row + 1, col, layer))

    for copy in loads:
        copy.wait()
    for i in range(blocks):
        for j in range(blocks):
            stored = pattern[row * blocks + i, col * blocks + j] == 1
            side, at = divmod(i, half_blocks)
            rows, cols = slice(at * BS, (at + 1) * BS), slice(j * BS, (j + 1) * BS)
            block = right[row, side, rows, cols]
            right[row, side, rows, cols] = jnp.where(stored, block, jnp.zeros_like(block))

    ends = (row > 0).astype(jnp.int32) + (row < n - 1).astype(jnp.int32)
    pl.semaphore_wait(barrier, n + ends)

    up_open = (row < n - 1) & ((col != n - 1) | (row != n - 2))
    down_open = (row > 0) & ((col != 0) | (row != 1))
    corner = row == col

    def part(k, side, p):
        return right.at[k, side, pl.ds(p * piece, piece)]

    def left_part(k, p):
        return left.at[k, pl.ds(p * piece, piece)]

    def remote(src, dst, send, recv, device):
        return pltpu.make_async_remote_copy(
            src, dst, send, recv, device_id=device, device_id_type=MESH
        )

    def upward(k, p):
        ref = part(k, layer, p)
        return remote(ref, ref, up_send.at[k, p], right_recv.at[k, p], (row + 1, col, layer))

    def downward(k, p):
        ref = part(k, layer, p)
        return remote(ref, ref, down_send.at[k, p], right_recv.at[k, p], (row - 1, col, layer))

    def across(k, p):
        ref = part(k, layer, p)
        return remote(ref, ref, sib_send.at[k, p], sib_recv.at[k, p], (row, col, other))

    def left_across(k, p):
        return remote(
            left_part(k, p), part(k, layer, p),
            sib_send.at[k, p], sib_recv.at[k, p], (row, col, other),
        )

    def from_across(k, p):
        ref = part(k, other, p)
        return remote(ref, ref, sib_send.at[k, p], sib_recv.at[k, p], (row, col, other))

    def along(target, p):
        return remote(
            part(row, layer, p), left_part(col, p),
            left_send.at[target, p], left_recv.at[col, p], (row, target, layer),
        )

    def relay(k, target, slot, p):
        return remote(
            left_part(k, p), left_part(k, p),
            pass_send.at[k, slot, p], left_recv.at[k, p], (row, target, layer),
        )

    beside = [my_y * wide + lax.rem(my_x + i, wide) for i in range(1, wide)]
    above = [lax.rem(my_y + i, tall) * wide + my_x for i in range(1, tall)]
    diagonal = [
        lax.rem(my_y + i, tall) * wide + lax.rem(my_x + j, wide)
        for i in range(1, tall) for j in range(1, wide)
    ]

    def is_even(k):
        return lax.rem(lax.div(k, wide) + lax.rem(k, wide), 2) == 0

    for p in range(PIECES):
        @pl.when(up_open)
        def _():
            upward(row, p).start()

        @pl.when(down_open)
        def _():
            downward(row, p).start()

        for target in beside + above:
            along(target, p).start()

    left[col] = right[row, layer]
    total[...] = jnp.zeros_like(total)

    def take_left(k, p):
        left_copy = relay(k, col, 0, p)
        left_copy.wait_recv()

        @pl.when(corner)
        def _():
            left_across(k, p).start()

    def take_near(p):
        for k in beside:
            take_left(k, p)

            @pl.when(is_even(k))
            def _():
                for slot, target in enumerate(above):
                    relay(k, target, slot, p).start()

        for k in above:
            take_left(k, p)

            @pl.when(jnp.logical_not(is_even(k)))
            def _():
                for slot, target in enumerate(beside):
                    relay(k, target, slot, p).start()

    def pass_on(step, p):
        @pl.when((row >= step) & ((col != n - 1) | (row != n - 1)))
        def _():
            k = row - step
            upward(k, p).wait_recv()

            @pl.when(up_open)
            def _():
                upward(k, p).start()

            @pl.when(jnp.logical_not(corner))
            def _():
                across(k, p).start()

        @pl.when((row + step < n) & ((col != 0) | (row != 0)))
        def _():
            k = row + step
            downward(k, p).wait_recv()

            @pl.when(down_open)
            def _():
                downward(k, p).start()

            @pl.when(jnp.logical_not(corner))
            def _():
                across(k, p).start()

    turned = (((1,), (1,)), ((), ()))

    def product(k, ref):
        return lax.dot_general(left[k], ref[...], turned, preferred_element_type=jnp.float32)

    def multiply(k):
        as_is = (k == row) | jnp.logical_not(corner)

        @pl.when(as_is)
        def _():
            for side in range(2):
                total[...] += jnp.dot(
                    left[k, :, side * half:(side + 1) * half], right[k, side],
                    preferred_element_type=jnp.float32,
                )

        @pl.when(jnp.logical_not(as_is))
        def _():
            total[:, pl.ds(pl.multiple_of(layer * half, half), half)] += product(k, left.at[k])
            total[:, pl.ds(pl.multiple_of(other * half, half), half)] += product(k, right.at[k, other])

    for p in range(PIECES):
        pass_on(1, p)
        take_near(p)
    for step in range(2, n):
        for p in range(PIECES):
            pass_on(step, p)
        if step == 2:
            for p in range(PIECES):
                for k in diagonal:
                    take_left(k, p)
            multiply(row)

    @pl.loop(1, n)
    def _(step):
        k = lax.rem(row + step, n)
        for p in range(PIECES):
            from_across(k, p).wait_recv()
        multiply(k)

    for i in range(half_blocks):
        for j in range(blocks):
            kept = keep[row * blocks + layer * half_blocks + i, col * blocks + j] == 1
            rows, cols = slice(i * BS, (i + 1) * BS), slice(j * BS, (j + 1) * BS)
            value = total[rows, cols]
            out[rows, cols] = jnp.where(kept, value, jnp.zeros_like(value)).astype(out.dtype)

    for p in range(PIECES):
        for target in beside + above:
            along(target, p).wait_send()
        for k in beside:
            @pl.when(is_even(k))
            def _():
                for slot, target in enumerate(above):
                    relay(k, target, slot, p).wait_send()

        for k in above:
            @pl.when(jnp.logical_not(is_even(k)))
            def _():
                for slot, target in enumerate(beside):
                    relay(k, target, slot, p).wait_send()

        for k in range(n):
            @pl.when(up_open & (k <= row))
            def _():
                upward(k, p).wait_send()

            @pl.when(down_open & (k >= row))
            def _():
                downward(k, p).wait_send()

            @pl.when(k != row)
            def _():
                across(k, p).wait_send()


def local(density, pattern, filter_pattern):
    grid = lax.axis_size("row")
    tile = density.shape[0]
    half = tile // 2
    dma = pltpu.SemaphoreType.DMA
    return pl.pallas_call(
        functools.partial(kernel, grid),
        out_shape=jax.ShapeDtypeStruct((half, tile), jnp.bfloat16),
        in_specs=[
            pl.BlockSpec(memory_space=pltpu.HBM),
            pl.BlockSpec(memory_space=pltpu.HBM),
            pl.BlockSpec(memory_space=pltpu.HBM),
        ],
        out_specs=pl.BlockSpec(memory_space=pltpu.VMEM),
        scratch_shapes=[
            pltpu.VMEM((grid, half, tile), jnp.bfloat16),
            pltpu.VMEM((grid, 2, half, tile), jnp.bfloat16),
            pltpu.VMEM((half, tile), jnp.float32),
            pltpu.SMEM(pattern.shape, pattern.dtype),
            pltpu.SMEM(filter_pattern.shape, filter_pattern.dtype),
            dma((grid, PIECES)),
            dma((grid, grid, PIECES)),
            dma((grid, PIECES)),
            dma((grid, PIECES)),
            dma((grid, PIECES)),
            dma((grid, PIECES)),
            dma((grid, PIECES)),
            dma((grid, PIECES)),
            dma((4,)),
        ],
        compiler_params=pltpu.CompilerParams(
            collective_id=0, has_side_effects=True, vmem_limit_bytes=63 * 1024 * 1024
        ),
    )(density, pattern, filter_pattern)


def solution(mesh):
    return jax.shard_map(
        local,
        mesh=mesh,
        in_specs=(P("row", "col"), P(), P()),
        out_specs=P(("row", "depth"), "col"),
        check_vma=False,
    )
```

```python
import functools

import jax
import jax.numpy as jnp
from jax import lax
from jax.experimental import pallas as pl
from jax.experimental.pallas import tpu as pltpu
from jax.sharding import PartitionSpec as P

BS = 256
PIECES = 2
MESH = pl.DeviceIdType.MESH


def kernel(n, density, pattern_ref, keep_ref, out, left, right, total, pattern, keep, *sems):
    (left_send, pass_send, left_recv, up_send, down_send, right_recv,
     sib_send, sib_recv, load) = sems
    row = lax.axis_index("row")
    col = lax.axis_index("col")
    layer = lax.axis_index("depth")
    other = 1 - layer
    tile = density.shape[0]
    blocks = tile // BS
    half = tile // 2
    half_blocks = half // BS
    piece = half // PIECES
    wide = max(w for w in range(1, n + 1) if n % w == 0 and w * w <= n)
    tall = n // wide
    my_y, my_x = lax.div(col, wide), lax.rem(col, wide)

    loads = [
        pltpu.make_async_copy(density.at[pl.ds(side * half, half)], right.at[row, side], load.at[side])
        for side in range(2)
    ]
    loads.append(pltpu.make_async_copy(pattern_ref, pattern, load.at[2]))
    loads.append(pltpu.make_async_copy(keep_ref, keep, load.at[3]))
    for copy in loads:
        copy.start()

    barrier = pltpu.get_barrier_semaphore()

    def greet(device):
        pl.semaphore_signal(barrier, inc=1, device_id=device, device_id_type=MESH)

    for step in range(1, n):
        greet((row, lax.rem(col + step, n), layer))
    greet((row, col, other))

    @pl.when(row > 0)
    def _():
        greet((row - 1, col, layer))

    @pl.when(row < n - 1)
    def _():
        greet((row + 1, col, layer))

    for copy in loads:
        copy.wait()
    for i in range(blocks):
        for j in range(blocks):
            stored = pattern[row * blocks + i, col * blocks + j] == 1
            side, at = divmod(i, half_blocks)
            rows, cols = slice(at * BS, (at + 1) * BS), slice(j * BS, (j + 1) * BS)
            block = right[row, side, rows, cols]
            right[row, side, rows, cols] = jnp.where(stored, block, jnp.zeros_like(block))

    ends = (row > 0).astype(jnp.int32) + (row < n - 1).astype(jnp.int32)
    pl.semaphore_wait(barrier, n + ends)

    up_open = (row < n - 1) & ((col != n - 1) | (row != n - 2))
    down_open = (row > 0) & ((col != 0) | (row != 1))
    corner = row == col

    def part(k, side, p):
        return right.at[k, side, pl.ds(p * piece, piece)]

    def left_part(k, p):
        return left.at[k, pl.ds(p * piece, piece)]

    def remote(src, dst, send, recv, device):
        return pltpu.make_async_remote_copy(
            src, dst, send, recv, device_id=device, device_id_type=MESH
        )

    def upward(k, p):
        ref = part(k, layer, p)
        return remote(ref, ref, up_send.at[k, p], right_recv.at[k, p], (row + 1, col, layer))

    def downward(k, p):
        ref = part(k, layer, p)
        return remote(ref, ref, down_send.at[k, p], right_recv.at[k, p], (row - 1, col, layer))

    def across(k, p):
        ref = part(k, layer, p)
        return remote(ref, ref, sib_send.at[k, p], sib_recv.at[k, p], (row, col, other))

    def left_across(k, p):
        return remote(
            left_part(k, p), part(k, layer, p),
            sib_send.at[k, p], sib_recv.at[k, p], (row, col, other),
        )

    def from_across(k, p):
        ref = part(k, other, p)
        return remote(ref, ref, sib_send.at[k, p], sib_recv.at[k, p], (row, col, other))

    def along(target, p):
        return remote(
            part(row, layer, p), left_part(col, p),
            left_send.at[target, p], left_recv.at[col, p], (row, target, layer),
        )

    def relay(k, target, slot, p):
        return remote(
            left_part(k, p), left_part(k, p),
            pass_send.at[k, slot, p], left_recv.at[k, p], (row, target, layer),
        )

    beside = [my_y * wide + lax.rem(my_x + i, wide) for i in range(1, wide)]
    above = [lax.rem(my_y + i, tall) * wide + my_x for i in range(1, tall)]
    diagonal = [
        lax.rem(my_y + i, tall) * wide + lax.rem(my_x + j, wide)
        for i in range(1, tall) for j in range(1, wide)
    ]

    def is_even(k):
        return lax.rem(lax.div(k, wide) + lax.rem(k, wide), 2) == 0

    for p in range(PIECES):
        @pl.when(up_open)
        def _():
            upward(row, p).start()

        @pl.when(down_open)
        def _():
            downward(row, p).start()

        for target in beside + above:
            along(target, p).start()

    left[col] = right[row, layer]
    total[...] = jnp.zeros_like(total)

    def take_left(k, p):
        left_copy = relay(k, col, 0, p)
        left_copy.wait_recv()

        @pl.when(corner)
        def _():
            left_across(k, p).start()

    def take_near(p):
        for k in beside:
            take_left(k, p)

            @pl.when(is_even(k))
            def _():
                for slot, target in enumerate(above):
                    relay(k, target, slot, p).start()

        for k in above:
            take_left(k, p)

            @pl.when(jnp.logical_not(is_even(k)))
            def _():
                for slot, target in enumerate(beside):
                    relay(k, target, slot, p).start()

    def pass_on(step, p):
        @pl.when((row >= step) & ((col != n - 1) | (row != n - 1)))
        def _():
            k = row - step
            upward(k, p).wait_recv()

            @pl.when(up_open)
            def _():
                upward(k, p).start()

            @pl.when(jnp.logical_not(corner))
            def _():
                across(k, p).start()

        @pl.when((row + step < n) & ((col != 0) | (row != 0)))
        def _():
            k = row + step
            downward(k, p).wait_recv()

            @pl.when(down_open)
            def _():
                downward(k, p).start()

            @pl.when(jnp.logical_not(corner))
            def _():
                across(k, p).start()

    turned = (((1,), (1,)), ((), ()))

    def product(k, ref):
        return lax.dot_general(left[k], ref[...], turned, preferred_element_type=jnp.float32)

    def multiply(k):
        as_is = (k == row) | jnp.logical_not(corner)

        @pl.when(as_is)
        def _():
            for side in range(2):
                total[...] += jnp.dot(
                    left[k, :, side * half:(side + 1) * half], right[k, side],
                    preferred_element_type=jnp.float32,
                )

        @pl.when(jnp.logical_not(as_is))
        def _():
            total[:, pl.ds(pl.multiple_of(layer * half, half), half)] += product(k, left.at[k])
            total[:, pl.ds(pl.multiple_of(other * half, half), half)] += product(k, right.at[k, other])

    def multiply_step(step):
        for k, there in ((row - step, row >= step), (row + step, row + step < n)):
            @pl.when(there)
            def _():
                for p in range(PIECES):
                    from_across(k, p).wait_recv()
                multiply(k)

    for p in range(PIECES):
        pass_on(1, p)
        take_near(p)
    for step in range(2, n):
        for p in range(PIECES):
            pass_on(step, p)
        if step == 2:
            for p in range(PIECES):
                for k in diagonal:
                    take_left(k, p)
            multiply(row)
        multiply_step(step - 1)

    multiply_step(n - 1)

    for i in range(half_blocks):
        for j in range(blocks):
            kept = keep[row * blocks + layer * half_blocks + i, col * blocks + j] == 1
            rows, cols = slice(i * BS, (i + 1) * BS), slice(j * BS, (j + 1) * BS)
            value = total[rows, cols]
            out[rows, cols] = jnp.where(kept, value, jnp.zeros_like(value)).astype(out.dtype)

    for p in range(PIECES):
        for target in beside + above:
            along(target, p).wait_send()
        for k in beside:
            @pl.when(is_even(k))
            def _():
                for slot, target in enumerate(above):
                    relay(k, target, slot, p).wait_send()

        for k in above:
            @pl.when(jnp.logical_not(is_even(k)))
            def _():
                for slot, target in enumerate(beside):
                    relay(k, target, slot, p).wait_send()

        for k in range(n):
            @pl.when(up_open & (k <= row))
            def _():
                upward(k, p).wait_send()

            @pl.when(down_open & (k >= row))
            def _():
                downward(k, p).wait_send()

            @pl.when(k != row)
            def _():
                across(k, p).wait_send()


def local(density, pattern, filter_pattern):
    grid = lax.axis_size("row")
    tile = density.shape[0]
    half = tile // 2
    dma = pltpu.SemaphoreType.DMA
    return pl.pallas_call(
        functools.partial(kernel, grid),
        out_shape=jax.ShapeDtypeStruct((half, tile), jnp.bfloat16),
        in_specs=[
            pl.BlockSpec(memory_space=pltpu.HBM),
            pl.BlockSpec(memory_space=pltpu.HBM),
            pl.BlockSpec(memory_space=pltpu.HBM),
        ],
        out_specs=pl.BlockSpec(memory_space=pltpu.VMEM),
        scratch_shapes=[
            pltpu.VMEM((grid, half, tile), jnp.bfloat16),
            pltpu.VMEM((grid, 2, half, tile), jnp.bfloat16),
            pltpu.VMEM((half, tile), jnp.float32),
            pltpu.SMEM(pattern.shape, pattern.dtype),
            pltpu.SMEM(filter_pattern.shape, filter_pattern.dtype),
            dma((grid, PIECES)),
            dma((grid, grid, PIECES)),
            dma((grid, PIECES)),
            dma((grid, PIECES)),
            dma((grid, PIECES)),
            dma((grid, PIECES)),
            dma((grid, PIECES)),
            dma((grid, PIECES)),
            dma((4,)),
        ],
        compiler_params=pltpu.CompilerParams(
            collective_id=0, has_side_effects=True, vmem_limit_bytes=63 * 1024 * 1024
        ),
    )(density, pattern, filter_pattern)


def solution(mesh):
    return jax.shard_map(
        local,
        mesh=mesh,
        in_specs=(P("row", "col"), P(), P()),
        out_specs=P(("row", "depth"), "col"),
        check_vma=False,
    )
```
